512 devices in a mesh: context: 128 (over z_lo, y, x, core), tensor: 4 (over z_hi).
Axes of the slice: x: 4, y: 4, z: 16 (z_hi: 4, z_lo: 4; z = z_hi * 4 + z_lo), core: 2. Of those that a mesh axis runs over, the one named last changes fastest.
Arguments:
- query_gate: bfloat16 [16384, 4096], P('context', 'tensor'), may hold values from -12 to 12
- key_branch: bfloat16 [16384, 4096], P('context', 'tensor'), may hold values from -6 to 6
- value_branch: bfloat16 [16384, 4096], P('context', 'tensor'), may hold values from -6 to 6
- filter_spectrum: float32 [128, 2, 2, 256, 128], P('context', None, None, 'tensor'), may hold values from -4 to 4, as said below
- norm_gain: bfloat16 [4096], P('tensor'), may hold values from 0.5 to 1.5
Outputs:
- gated_mix: float32 [16384, 4096], P('context', 'tensor')
- normed: bfloat16 [16384, 4096], P('context', 'tensor')
The draws below stay inside these ranges and needn't reach their ends.
Inputs may be any that keep to these rules, and one draw needn't show every extreme that they name: `filter_spectrum`: every group's response is that of a real filter: response_g[32768 - k] is the complex conjugate of response_g[k] (indices modulo 32768).
All inputs are finite; a program needn't handle non-finite values.
Results may differ from the reference program's by a relative error of at most 0.001.
Values sent between devices are 32-bit elements; how exact they have to be, the bound alone decides.
A program may use at most 64 MiB of HBM per device.

```python
import math
import jax
import jax.numpy as jnp
import numpy as np
from jax import lax

CHANNELS = 4096
GROUP = 16
TOK_DEV = 128
TOKENS = 16384
GROUPS = 256
FREQS = 32768
N_CONTEXT = 128


def reversed_positions(number):
    places = number.bit_length() - 1
    series = jnp.arange(number, dtype=jnp.int32)
    flipped = jnp.zeros(number, jnp.int32)
    for position in range(places):
        flipped = flipped + (series >> position & 1) * (1 << places - 1 - position)
    return flipped


def draw_query_gate(key, part):
    key = jax.random.fold_in(key, 5)
    first_key, second_key = jax.random.split(key, 2)
    pattern = jax.random.truncated_normal(first_key, -4.0, 4.0, (TOKENS, CHANNELS), jnp.float32)
    columns = jnp.exp(jax.random.uniform(second_key, (1, CHANNELS), jnp.float32, math.log(0.3), math.log(3.0)))
    slope = 1.0 + jnp.arange(CHANNELS, dtype=jnp.float32) / CHANNELS
    return jnp.clip(pattern * columns * slope[None, :], -12.0, 12.0).astype(jnp.bfloat16)


def draw_filter_spectrum(key, part):
    key = jax.random.fold_in(key, 11)
    first_key = jax.random.fold_in(key, 0)
    contexts = FREQS // (2 * TOK_DEV)
    raw = jax.random.normal(first_key, (2, GROUPS, FREQS), jnp.float32)
    mirror = (FREQS - jnp.arange(FREQS, dtype=jnp.int32)) % FREQS
    mirrored = raw[:, :, mirror]
    real_part = (raw[0] + mirrored[0]) * 0.7
    imag_part = (raw[1] - mirrored[1]) * 0.7
    natural = jnp.clip(jnp.stack([real_part, imag_part]), -4.0, 4.0)
    flipped = reversed_positions(contexts)
    column = jnp.arange(2, dtype=jnp.int32)[None, :, None] + 2 * flipped[:, None, None] + 2 * contexts * jnp.arange(TOK_DEV, dtype=jnp.int32)[None, None, :]
    picked = natural[:, :, column]
    return jnp.transpose(picked, (2, 0, 3, 1, 4))


def shard_levels(own_key, shape, shards, least, top_value):
    gain = 1.0
    for dim, parts in shards:
        steps = jax.random.uniform(jax.random.fold_in(jax.random.fold_in(own_key, 6), dim), (parts,), jnp.float32, least / len(shards), top_value / len(shards))
        gain = gain * jnp.repeat(jnp.exp(steps), shape[dim] // parts).reshape((-1,) + (1,) * (len(shape) - 1 - dim))
    return gain


def normal_values(stream_key, shape, spread, reach, shards=(), kind=jnp.bfloat16):
    level = shard_levels(stream_key, shape, shards, -0.22, 0.18) if shards else 1.0
    entries = jax.random.normal(stream_key, shape, jnp.float32) * spread * level
    return jnp.minimum(jnp.maximum(entries, -reach), reach).astype(kind)


def setup_inputs(seed: int = 0) -> dict:
    key_list = jax.random.split(jax.random.key(seed), 6)
    return {
        "query_gate": draw_query_gate(jax.random.fold_in(key_list[5], 71), 0),
        "key_branch": normal_values(key_list[1], (TOKENS, CHANNELS), 1.0, 6.0, ((0, 128), (1, 4))),
        "value_branch": normal_values(key_list[2], (TOKENS, CHANNELS), 1.0, 6.0, ((0, 128), (1, 4))),
        "filter_spectrum": draw_filter_spectrum(jax.random.fold_in(key_list[5], 71), 0),
        "norm_gain": jnp.clip(1.0 + 0.1 * jax.random.normal(key_list[4], (CHANNELS,), jnp.float32), 0.5, 1.5).astype(jnp.bfloat16),
    }


EPSILON = 1e-06

def reversal_table(number):
    places = number.bit_length() - 1
    result = np.zeros(number, dtype=np.int32)
    for member in range(number):
        flipped = 0
        for position in range(places):
            if member >> position & 1:
                flipped = flipped | 1 << places - 1 - position
        result[member] = flipped
    return result

def reference(query_gate, key_branch, value_branch, filter_spectrum, norm_gain):
    driven = key_branch.astype(jnp.float32) * value_branch.astype(jnp.float32)
    ordered = filter_spectrum[reversal_table(N_CONTEXT)]
    natural = jnp.transpose(ordered, (1, 3, 4, 0, 2)).reshape(2, GROUPS, FREQS)
    half_count = FREQS // 2 + 1
    per_block = math.gcd(GROUPS, 16)
    blocks = GROUPS // per_block
    signal = driven.reshape(TOKENS, blocks, per_block, GROUP).transpose(1, 0, 2, 3)
    filter_re = natural[0, :, :half_count].reshape(blocks, per_block, half_count)
    filter_im = natural[1, :, :half_count].reshape(blocks, per_block, half_count)

    def convolve(pieces):
        segment, part_re, part_im = pieces
        transformed = jnp.fft.rfft(segment, n=FREQS, axis=0)
        response = lax.complex(part_re, part_im).T[:, :, None]
        return jnp.fft.irfft(transformed * response, n=FREQS, axis=0)[:TOKENS]
    convolved = lax.map(convolve, (signal, filter_re, filter_im))
    convolved = convolved.transpose(1, 0, 2, 3).reshape(TOKENS, CHANNELS)
    gated_mix = query_gate.astype(jnp.float32) * convolved
    mean_square = lax.optimization_barrier(jnp.sum(gated_mix * gated_mix, axis=1, keepdims=True)) / CHANNELS
    normed = (gated_mix * lax.rsqrt(mean_square + EPSILON) * norm_gain.astype(jnp.float32)).astype(jnp.bfloat16)
    return (gated_mix, normed)
```

```python
import functools

import jax
import jax.numpy as jnp
import ml_dtypes
import numpy as np
from jax import lax
from jax.experimental import pallas as pl
from jax.experimental.pallas import tpu as pltpu
from jax.sharding import PartitionSpec as P

MESH = pl.DeviceIdType.MESH
F32, BF16 = jnp.float32, jnp.bfloat16

CHANNELS = 4096
TOK = 128
CTX = 128
TEN = 4
FREQS = 2 * TOK * CTX
LOCAL = CHANNELS // TEN
OWN = LOCAL // CTX
PARTS = 1
PC = OWN // PARTS
HALF = CTX // 2
LOW = 8
HIGH = CTX // LOW
EPSILON = 1e-06


def two_terms(table):
    high = table.astype(ml_dtypes.bfloat16)
    low = (table - high.astype(np.float64)).astype(ml_dtypes.bfloat16)
    return high, low


def tables():
    f = np.concatenate([np.arange(0, CTX, 2), np.arange(1, CTX, 2)]).astype(np.float64)
    a = np.arange(CTX, dtype=np.float64)
    first = 2 * np.pi * f[:, None] * a[None, :] / (2 * CTX)
    forward_a = np.concatenate([np.cos(first), -np.sin(first)], axis=0)
    a_high, a_low = two_terms(forward_a)
    a_high = np.concatenate([a_high, a_high], axis=1)
    twist = 2 * np.pi * f[:, None] * a[None, :] / FREQS
    weight = np.where(f == 0, 1.0, 2.0)[:, None] / FREQS
    edge = 2 * np.pi * CTX * a / FREQS
    turn = np.stack([np.cos(twist), np.sin(twist), np.cos(twist) * weight, np.sin(twist) * weight])
    edges = np.stack([np.cos(edge), np.sin(edge), np.cos(edge) / FREQS, np.sin(edge) / FREQS])
    edges = np.repeat(edges[:, None, :], 16, axis=1)
    second = 2 * np.pi * a[:, None] * a[None, :] / TOK
    cos, sin = np.cos(second), np.sin(second)
    forward_j = two_terms(np.block([[cos, -sin], [sin, cos]]))
    inverse_j = two_terms(np.block([[cos, sin], [-sin, cos]]))
    inverse_a = two_terms(np.concatenate([np.cos(first.T), -np.sin(first.T)], axis=1))
    sign = np.repeat(np.where(a % 2 == 0, 1.0, -1.0)[:, None], TOK, axis=1)
    return (
        a_high,
        a_low,
        turn.astype(np.float32),
        edges.astype(np.float32),
        np.stack(forward_j),
        np.stack(inverse_j),
        np.concatenate(inverse_a, axis=0),
        sign.astype(np.float32),
    )


def split(value):
    high = value.astype(BF16)
    return high, (value - high.astype(F32)).astype(BF16)


def dot(left, right):
    return jnp.dot(left, right, preferred_element_type=F32)


def three_products(value, pair):
    rows = value.shape[0]
    high, low = split(value)
    both = dot(jnp.concatenate([high, low], axis=0), pair[0])
    return both[:rows] + both[rows:] + dot(high, pair[1])


def reversed_index(position):
    flipped = 0
    for place in range(7):
        flipped = flipped + ((position >> place) & 1) * (1 << (6 - place))
    return flipped


def mixer(
    query, key, value, spectrum, a_fwd, a_low, turn, edges, j_fwd, j_inv, a_inv, sign,
    gated, scale,
    sending, arrived, answer, result, query_t, pieces, response, squares,
    send_sem, recv_sem, back_send, back_recv, filt_send, filt_recv, sq_send, sq_recv, own_sem, ready,
):
    me = lax.axis_index("context")
    mine = lax.axis_index("tensor")
    my_high, my_low = me // LOW, me % LOW

    def device(high, low):
        return (my_high ^ high) * LOW + (my_low ^ low)

    barrier = pltpu.get_barrier_semaphore()
    for low in range(1, LOW):
        pl.semaphore_signal(barrier, inc=1, device_id=(device(0, low), mine), device_id_type=MESH)
    for high in range(1, HIGH):
        pl.semaphore_signal(barrier, inc=1, device_id=(device(high, 0), mine), device_id_type=MESH)
    for step in range(1, TEN):
        pl.semaphore_signal(barrier, inc=1, device_id=(me, mine ^ step), device_id_type=MESH)

    for block in range(LOCAL // 128):
        columns = pl.ds(block * 128, 128)
        driven = key[:, columns].astype(F32) * value[:, columns].astype(F32)
        sending[columns, :] = driven.T

    pl.semaphore_wait(barrier, LOW - 1 + HIGH - 1 + TEN - 1)
    for low in range(1, LOW):
        pl.semaphore_signal(ready.at[low], inc=1, device_id=(device(0, low), mine), device_id_type=MESH)

    def rows_of(start, count):
        return pl.ds(pl.multiple_of(start * count, count), count)

    def exchange(part, low, first):
        def step(high, carry):
            target = device(high, low)
            pltpu.make_async_remote_copy(
                src_ref=sending.at[rows_of(target * PARTS + part, PC)],
                dst_ref=arrived.at[part, rows_of(me, PC)],
                send_sem=send_sem.at[part],
                recv_sem=recv_sem.at[part],
                device_id=(target, mine),
                device_id_type=MESH,
            ).start()
            return carry

        lax.fori_loop(first, HIGH, step, 0)

    own = [
        pltpu.make_async_copy(
            sending.at[rows_of(me * PARTS + part, PC)], arrived.at[part, rows_of(me, PC)], own_sem.at[part]
        )
        for part in range(PARTS)
    ]
    for part in range(PARTS):
        own[part].start()
        for low in range(LOW):
            if low and not part:
                pl.semaphore_wait(ready.at[low], 1)
            exchange(part, low, 0 if low else 1)

    order = reversed_index(me)
    holds = order <= HALF
    for kind in range(4):
        pieces[pl.ds(kind, LOCAL // 16, stride=4), :] = spectrum[kind // 2, kind % 2]

    def filter_copy(target):
        return pltpu.make_async_remote_copy(
            src_ref=pieces.at[rows_of(target // 2, 4)],
            dst_ref=response.at[rows_of(order, 4)],
            send_sem=filt_send,
            recv_sem=filt_recv,
            device_id=(target, mine),
            device_id_type=MESH,
        )

    @pl.when(holds)
    def _():
        def step(other, carry):
            filter_copy(me ^ other).start()
            return carry

        lax.fori_loop(1, CTX, step, 0)
        local = pltpu.make_async_copy(
            pieces.at[rows_of(me // 2, 4)], response.at[rows_of(order, 4)], own_sem.at[PARTS]
        )
        local.start()
        local.wait()

    for block in range(LOCAL // 128):
        columns = pl.ds(block * 128, 128)
        query_t[columns, :] = query[:, columns].astype(F32).T

    def wait_rows(ref, count, sem):
        pltpu.make_async_copy(ref.at[pl.ds(0, count)], ref.at[pl.ds(0, count)], sem).wait()

    for part in range(PARTS):
        own[part].wait()
        wait_rows(arrived.at[part], (CTX - 1) * PC, recv_sem.at[part])

        block = arrived[part].reshape(CTX // 2, 2 * PC, TOK)
        folded = jnp.sum(block, axis=0)
        edge = folded[:PC] - folded[PC:]
        edge = jnp.concatenate([edge, jnp.zeros((16 - PC, TOK), F32)], axis=0)
        edge = jnp.concatenate([edge * edges[0], -edge * edges[1]], axis=1)
        edge = three_products(edge, j_fwd)

        if part == 0:

            @pl.when(holds)
            def _():
                wait_rows(response, HALF * 4, filt_recv)

            @pl.when(jnp.logical_not(holds))
            def _():
                wait_rows(response, (HALF + 1) * 4, filt_recv)

        h_re = jnp.concatenate([response[pl.ds(kind, HALF, stride=4), :] for kind in (0, 1)], axis=0)
        h_im = jnp.concatenate([response[pl.ds(kind, HALF, stride=4), :] for kind in (2, 3)], axis=0)
        e_re, e_im = response[pl.ds(4 * HALF, 1), :], response[pl.ds(4 * HALF + 2, 1), :]
        z_re, z_im = edge[:, :TOK], edge[:, TOK:]
        edge = jnp.concatenate([z_re * e_re - z_im * e_im, z_re * e_im + z_im * e_re], axis=1)
        edge = three_products(edge, j_inv)
        edge = edge[:, :TOK] * edges[2] - edge[:, TOK:] * edges[3]

        for pair in range(PC // 2):
            high, low = split(
                jnp.concatenate(
                    [arrived[part, pl.ds(2 * pair + k, CTX, stride=PC), :] for k in (0, 1)], axis=1
                )
            )
            freq = dot(a_fwd[...], jnp.concatenate([high, low], axis=0)) + dot(a_low[...], high)
            rows = []
            for k in (0, 1):
                y_re, y_im = freq[:CTX, k * TOK : (k + 1) * TOK], freq[CTX:, k * TOK : (k + 1) * TOK]
                rows.append(
                    jnp.concatenate([y_re * turn[0] + y_im * turn[1], y_im * turn[0] - y_re * turn[1]], axis=1)
                )
            freq = three_products(jnp.concatenate(rows, axis=0), j_fwd)
            rows = []
            for k in (0, 1):
                z_re, z_im = freq[k * CTX : (k + 1) * CTX, :TOK], freq[k * CTX : (k + 1) * CTX, TOK:]
                rows.append(jnp.concatenate([z_re * h_re - z_im * h_im, z_re * h_im + z_im * h_re], axis=1))
            back = three_products(jnp.concatenate(rows, axis=0), j_inv)
            columns = []
            for k in (0, 1):
                u_re, u_im = back[k * CTX : (k + 1) * CTX, :TOK], back[k * CTX : (k + 1) * CTX, TOK:]
                columns.append(
                    jnp.concatenate([u_re * turn[2] - u_im * turn[3], u_im * turn[2] + u_re * turn[3]], axis=0)
                )
            high, low = split(jnp.concatenate(columns, axis=1))
            both = dot(a_inv[...], high)
            back = both[:CTX] + both[CTX:] + dot(a_inv[:CTX], low)
            for k in (0, 1):
                channel = 2 * pair + k
                answer[part, pl.ds(channel, CTX, stride=PC), :] = (
                    back[:, k * TOK : (k + 1) * TOK] + sign[...] * edge[channel : channel + 1]
                )

        def step(other, carry):
            target = me ^ other
            pltpu.make_async_remote_copy(
                src_ref=answer.at[part, rows_of(target, PC)],
                dst_ref=result.at[rows_of(me * PARTS + part, PC)],
                send_sem=back_send,
                recv_sem=back_recv,
                device_id=(target, mine),
                device_id_type=MESH,
            ).start()
            return carry

        lax.fori_loop(1, CTX, step, 0)
        local = pltpu.make_async_copy(
            answer.at[part, rows_of(me, PC)], result.at[rows_of(me * PARTS + part, PC)], own_sem.at[part]
        )
        local.start()
        local.wait()

    wait_rows(result, (CTX - 1) * OWN, back_recv)
    total = jnp.zeros((8, TOK), F32)
    for block in range(LOCAL // 128):
        rows = pl.ds(block * 128, 128)
        mix = query_t[rows, :] * result[rows, :]
        gated[rows, :] = mix
        total = total + jnp.sum((mix * mix).reshape(16, 8, TOK), axis=0)
    squares[mine] = jnp.broadcast_to(jnp.sum(total, axis=0, keepdims=True), (8, TOK))
    copies = [
        pltpu.make_async_remote_copy(
            src_ref=squares.at[mine],
            dst_ref=squares.at[mine],
            send_sem=sq_send.at[step],
            recv_sem=sq_recv.at[step],
            device_id=(me, mine ^ step),
            device_id_type=MESH,
        )
        for step in range(1, TEN)
    ]
    for copy in copies:
        copy.start()
    for part in range(PARTS):
        wait_rows(sending, (CTX - 1) * PC, send_sem.at[part])
    wait_rows(sending, (CTX - 1) * OWN, back_send)

    @pl.when(holds)
    def _():
        wait_rows(sending, (CTX - 1) * 4, filt_send)

    for copy in copies:
        copy.wait()
    mean = (squares[0] + squares[1] + squares[2] + squares[3]) / CHANNELS
    scale[...] = lax.rsqrt(mean + EPSILON)


def finish(mixed, scale, gain, gated, normed):
    column = scale[...].T[:, 0:1]
    value = mixed[...].T
    gated[...] = value
    normed[...] = (value * column * gain[...].astype(F32)).astype(BF16)


def on_device(query_gate, key_branch, value_branch, filter_spectrum, norm_gain):
    vmem = pl.BlockSpec(memory_space=pltpu.VMEM)
    constants = [jnp.asarray(table) for table in tables()]
    mixed, scale = pl.pallas_call(
        mixer,
        out_shape=(
            jax.ShapeDtypeStruct((LOCAL, TOK), F32),
            jax.ShapeDtypeStruct((8, TOK), F32),
        ),
        in_specs=[vmem] * (4 + len(constants)),
        out_specs=(vmem, vmem),
        scratch_shapes=[
            pltpu.VMEM((LOCAL, TOK), F32),
            pltpu.VMEM((PARTS, CTX * PC, TOK), F32),
            pltpu.VMEM((PARTS, CTX * PC, TOK), F32),
            pltpu.VMEM((LOCAL, TOK), F32),
            pltpu.VMEM((LOCAL, TOK), F32),
            pltpu.VMEM((LOCAL // 16 * 4, TOK), F32),
            pltpu.VMEM(((HALF + 2) * 4, TOK), F32),
            pltpu.VMEM((TEN, 8, TOK), F32),
            pltpu.SemaphoreType.DMA((PARTS,)),
            pltpu.SemaphoreType.DMA((PARTS,)),
            pltpu.SemaphoreType.DMA,
            pltpu.SemaphoreType.DMA,
            pltpu.SemaphoreType.DMA,
            pltpu.SemaphoreType.DMA,
            pltpu.SemaphoreType.DMA((TEN,)),
            pltpu.SemaphoreType.DMA((TEN,)),
            pltpu.SemaphoreType.DMA((PARTS + 1,)),
            pltpu.SemaphoreType.REGULAR((LOW,)),
        ],
        compiler_params=pltpu.CompilerParams(
            collective_id=0, has_side_effects=True, vmem_limit_bytes=48 << 20
        ),
    )(query_gate, key_branch, value_branch, filter_spectrum.reshape(2, 2, -1, TOK), *constants)
    blocks = 4
    wide = LOCAL // blocks
    return pl.pallas_call(
        finish,
        grid=(blocks,),
        out_shape=(
            jax.ShapeDtypeStruct((TOK, LOCAL), F32),
            jax.ShapeDtypeStruct((TOK, LOCAL), BF16),
        ),
        in_specs=[
            pl.BlockSpec((wide, TOK), lambda i: (i, 0)),
            pl.BlockSpec((8, TOK), lambda i: (0, 0)),
            pl.BlockSpec((1, wide), lambda i: (0, i)),
        ],
        out_specs=(
            pl.BlockSpec((TOK, wide), lambda i: (0, i)),
            pl.BlockSpec((TOK, wide), lambda i: (0, i)),
        ),
        compiler_params=pltpu.CompilerParams(vmem_limit_bytes=16 << 20),
    )(mixed, scale, norm_gain.reshape(1, LOCAL))


def solution(mesh):
    placed = (
        P("context", "tensor"),
        P("context", "tensor"),
        P("context", "tensor"),
        P("context", None, None, "tensor", None),
        P("tensor"),
    )
    return jax.shard_map(
        on_device,
        mesh=mesh,
        in_specs=placed,
        out_specs=(P("context", "tensor"), P("context", "tensor")),
        check_vma=False,
    )
```

```python
import functools

import jax
import jax.numpy as jnp
import numpy as np
from jax import lax
from jax.experimental import pallas as pl
from jax.experimental.pallas import tpu as pltpu
from jax.sharding import PartitionSpec as P

MESH = pl.DeviceIdType.MESH
F32, BF16 = jnp.float32, jnp.bfloat16

CHANNELS = 4096
TOK = 128
CTX = 128
TEN = 4
FREQS = 2 * TOK * CTX
LOCAL = CHANNELS // TEN
OWN = LOCAL // CTX
PARTS = 1
PC = OWN // PARTS
HALF = CTX // 2
LOW = 8
HIGH = CTX // LOW
EPSILON = 1e-06


def tables():
    f = np.concatenate([np.arange(0, CTX, 2), np.arange(1, CTX, 2)]).astype(np.float64)
    a = np.arange(CTX, dtype=np.float64)
    first = 2 * np.pi * f[:, None] * a[None, :] / (2 * CTX)
    twist = 2 * np.pi * f[:, None] * a[None, :] / FREQS
    weight = np.where(f == 0, 1.0, 2.0)[:, None] / FREQS
    edge = 2 * np.pi * CTX * a / FREQS
    turn = np.stack([np.cos(twist), np.sin(twist), np.cos(twist) * weight, np.sin(twist) * weight])
    edges = np.stack([np.cos(edge), np.sin(edge), np.cos(edge) / FREQS, np.sin(edge) / FREQS])
    edges = np.repeat(edges[:, None, :], 16, axis=1)
    second = 2 * np.pi * a[:, None] * a[None, :] / TOK
    cos, sin = np.cos(second), np.sin(second)
    forward_a = np.concatenate([np.cos(first), -np.sin(first)], axis=0)
    forward_j = np.block([[cos, -sin], [sin, cos]])
    inverse_j = np.block([[cos, sin], [-sin, cos]])
    sign = np.repeat(np.where(a % 2 == 0, 1.0, -1.0)[:, None], TOK, axis=1)
    square = np.concatenate([forward_j, inverse_j, forward_a.T], axis=0)
    narrow = np.concatenate([turn.reshape(-1, TOK), edges.reshape(-1, TOK), sign, forward_a], axis=0)
    return square.astype(np.float32), narrow.astype(np.float32)


def split(value):
    high = value.astype(BF16)
    return high, (value - high.astype(F32)).astype(BF16)


def dot(left, right):
    return jnp.dot(left, right, preferred_element_type=F32)


def three_products(value, pair):
    rows = value.shape[0]
    high, low = split(value)
    both = dot(jnp.concatenate([high, low], axis=0), pair[0])
    return both[:rows] + both[rows:] + dot(high, pair[1])


def reversed_index(position):
    flipped = 0
    for place in range(7):
        flipped = flipped + ((position >> place) & 1) * (1 << (6 - place))
    return flipped


def mixer(
    query_hbm, key_hbm, value_hbm, spectrum_hbm, square_hbm, narrow_hbm, gain_hbm,
    gated, scale, gain,
    query, key, value, spectrum, square, narrow, load_sem, a_fwd, a_low, j_fwd, j_inv, a_inv,
    sending, arrived, answer, result, query_t, pieces, response, transformed, squares,
    send_sem, recv_sem, back_send, back_recv, filt_send, filt_recv, hand_sem, sq_send, sq_recv, own_sem, ready,
):
    me = lax.axis_index("context")
    mine = lax.axis_index("tensor")
    my_high, my_low = me // LOW, me % LOW

    def device(high, low):
        return (my_high ^ high) * LOW + (my_low ^ low)

    loads = [
        pltpu.make_async_copy(source, target, load_sem.at[number])
        for number, (source, target) in enumerate(
            [
                (key_hbm, key),
                (value_hbm, value),
                (spectrum_hbm, spectrum),
                (query_hbm, query),
                (square_hbm, square),
                (narrow_hbm, narrow),
                (gain_hbm, gain),
            ]
        )
    ]
    for load in loads:
        load.start()
    turn = [narrow.at[pl.ds(TOK * k, TOK)] for k in range(4)]
    edges = [narrow.at[pl.ds(4 * TOK + 16 * k, 16)] for k in range(4)]
    sign = narrow.at[pl.ds(4 * TOK + 64, TOK)]

    barrier = pltpu.get_barrier_semaphore()
    for high in range(HIGH - 1, 0, -1):
        pl.semaphore_signal(barrier, inc=1, device_id=(device(high, 0), mine), device_id_type=MESH)
    for step in (1, 3):
        pl.semaphore_signal(barrier, inc=1, device_id=(me, mine ^ step), device_id_type=MESH)
    for low in range(LOW - 1, 0, -1):
        pl.semaphore_signal(barrier, inc=1, device_id=(device(0, low), mine), device_id_type=MESH)

    loads[0].wait()
    loads[1].wait()
    for block in range(LOCAL // 128):
        columns = pl.ds(block * 128, 128)
        driven = key[:, columns].astype(F32) * value[:, columns].astype(F32)
        sending[columns, :] = driven.T

    pl.semaphore_wait(barrier, LOW - 1 + HIGH - 1 + 2)
    pl.semaphore_signal(ready.at[0], inc=1, device_id=(me, mine ^ 1), device_id_type=MESH)
    for low in range(LOW - 1, 0, -1):
        pl.semaphore_signal(ready.at[low], inc=1, device_id=(device(0, low), mine), device_id_type=MESH)

    def rows_of(start, count):
        return pl.ds(pl.multiple_of(start * count, count), count)

    def exchange(part, low, first):
        def step(high, carry):
            target = device(high, low)
            pltpu.make_async_remote_copy(
                src_ref=sending.at[rows_of(target * PARTS + part, PC)],
                dst_ref=arrived.at[part, rows_of(me, PC)],
                send_sem=send_sem.at[part],
                recv_sem=recv_sem.at[part],
                device_id=(target, mine),
                device_id_type=MESH,
            ).start()
            return carry

        lax.fori_loop(first, HIGH, step, 0)

    own = [
        pltpu.make_async_copy(
            sending.at[rows_of(me * PARTS + part, PC)], arrived.at[part, rows_of(me, PC)], own_sem.at[part]
        )
        for part in range(PARTS)
    ]
    for part in range(PARTS):
        own[part].start()
        for low in range(LOW):
            if low and not part:
                pl.semaphore_wait(ready.at[low], 1)
            exchange(part, low, 0 if low else 1)

    order = reversed_index(me)
    loads[2].wait()
    for kind in range(4):
        pieces[pl.ds(kind, LOCAL // 16, stride=4), :] = spectrum[kind // 2, kind % 2]

    def filter_copy(chip):
        return pltpu.make_async_remote_copy(
            src_ref=pieces.at[rows_of(chip, 4)],
            dst_ref=response.at[rows_of(order, 4)],
            send_sem=filt_send,
            recv_sem=filt_recv,
            device_id=(2 * chip, mine),
            device_id_type=MESH,
        )

    first_core = me % 2 == 0
    hand_on = pltpu.make_async_remote_copy(
        src_ref=response.at[pl.ds(0, 4 * HALF + 4)],
        dst_ref=response.at[pl.ds(0, 4 * HALF + 4)],
        send_sem=hand_sem,
        recv_sem=filt_recv,
        device_id=(me ^ 1, mine),
        device_id_type=MESH,
    )

    @pl.when(first_core)
    def _():
        def step(other, carry):
            filter_copy((me // 2) ^ other).start()
            return carry

        lax.fori_loop(1, CTX // 2, step, 0)
        local = pltpu.make_async_copy(
            pieces.at[rows_of(me // 2, 4)], response.at[rows_of(order, 4)], own_sem.at[PARTS]
        )
        local.start()
        local.wait()

    @pl.when(order == HALF)
    def _():
        def step(chip, carry):
            filter_copy(chip).start()
            return carry

        lax.fori_loop(0, CTX // 2, step, 0)

    loads[3].wait()
    for block in range(LOCAL // 128):
        columns = pl.ds(block * 128, 128)
        query_t[columns, :] = query[:, columns].astype(F32).T

    def wait_rows(ref, count, sem):
        pltpu.make_async_copy(ref.at[pl.ds(0, count)], ref.at[pl.ds(0, count)], sem).wait()

    loads[4].wait()
    loads[5].wait()
    loads[6].wait()
    for target, first in ((j_fwd, 0), (j_inv, 256)):
        target[0], target[1] = split(square[pl.ds(first, 256), :])
    a_inv[pl.ds(0, CTX), :], a_inv[pl.ds(CTX, CTX), :] = split(square[pl.ds(512, CTX), :])
    high, low = split(narrow[pl.ds(5 * TOK + 64, 256), :])
    a_fwd[:, :CTX], a_fwd[:, CTX:], a_low[...] = high, high, low
    for part in range(PARTS):
        own[part].wait()
        wait_rows(arrived.at[part], (CTX - 1) * PC, recv_sem.at[part])

        if part == 0:

            @pl.when(first_core)
            def _():
                wait_rows(response, HALF * 4, filt_recv)
                hand_on.start()

        block = arrived[part].reshape(CTX // 2, 2 * PC, TOK)
        folded = jnp.sum(block, axis=0)
        edge = folded[:PC] - folded[PC:]
        edge = jnp.concatenate([edge, jnp.zeros((16 - PC, TOK), F32)], axis=0)
        edge = jnp.concatenate([edge * edges[0][...], -edge * edges[1][...]], axis=1)
        edge = three_products(edge, j_fwd)

        for pair in range(PC // 2):
            high, low = split(
                jnp.concatenate(
                    [arrived[part, pl.ds(2 * pair + k, CTX, stride=PC), :] for k in (0, 1)], axis=1
                )
            )
            freq = dot(a_fwd[...], jnp.concatenate([high, low], axis=0)) + dot(a_low[...], high)
            rows = []
            for k in (0, 1):
                y_re, y_im = freq[:CTX, k * TOK : (k + 1) * TOK], freq[CTX:, k * TOK : (k + 1) * TOK]
                rows.append(
                    jnp.concatenate(
                        [y_re * turn[0][...] + y_im * turn[1][...], y_im * turn[0][...] - y_re * turn[1][...]],
                        axis=1,
                    )
                )
            transformed[pair] = three_products(jnp.concatenate(rows, axis=0), j_fwd)

        if part == 0:

            @pl.when(jnp.logical_not(first_core))
            def _():
                wait_rows(response, (HALF + 1) * 4, filt_recv)

        h_re = jnp.concatenate([response[pl.ds(kind, HALF, stride=4), :] for kind in (0, 1)], axis=0)
        h_im = jnp.concatenate([response[pl.ds(kind, HALF, stride=4), :] for kind in (2, 3)], axis=0)
        e_re, e_im = response[pl.ds(4 * HALF, 1), :], response[pl.ds(4 * HALF + 2, 1), :]
        z_re, z_im = edge[:, :TOK], edge[:, TOK:]
        edge = jnp.concatenate([z_re * e_re - z_im * e_im, z_re * e_im + z_im * e_re], axis=1)
        edge = three_products(edge, j_inv)
        edge = edge[:, :TOK] * edges[2][...] - edge[:, TOK:] * edges[3][...]

        for pair in range(PC // 2):
            rows = []
            for k in (0, 1):
                z_re = transformed[pair, pl.ds(k * CTX, CTX), pl.ds(0, TOK)]
                z_im = transformed[pair, pl.ds(k * CTX, CTX), pl.ds(TOK, TOK)]
                rows.append(jnp.concatenate([z_re * h_re - z_im * h_im, z_re * h_im + z_im * h_re], axis=1))
            back = three_products(jnp.concatenate(rows, axis=0), j_inv)
            columns = []
            for k in (0, 1):
                u_re, u_im = back[k * CTX : (k + 1) * CTX, :TOK], back[k * CTX : (k + 1) * CTX, TOK:]
                columns.append(
                    jnp.concatenate(
                        [u_re * turn[2][...] - u_im * turn[3][...], u_im * turn[2][...] + u_re * turn[3][...]],
                        axis=0,
                    )
                )
            high, low = split(jnp.concatenate(columns, axis=1))
            both = dot(a_inv[...], high)
            back = both[:CTX] + both[CTX:] + dot(a_inv[pl.ds(0, CTX), :], low)
            for k in (0, 1):
                channel = 2 * pair + k
                answer[part, pl.ds(channel, CTX, stride=PC), :] = (
                    back[:, k * TOK : (k + 1) * TOK] + sign[...] * edge[channel : channel + 1]
                )

        def step(other, carry):
            target = (me + other) % CTX
            pltpu.make_async_remote_copy(
                src_ref=answer.at[part, rows_of(target, PC)],
                dst_ref=result.at[rows_of(me * PARTS + part, PC)],
                send_sem=back_send,
                recv_sem=back_recv,
                device_id=(target, mine),
                device_id_type=MESH,
            ).start()
            return carry

        lax.fori_loop(1, CTX, step, 0)
        local = pltpu.make_async_copy(
            answer.at[part, rows_of(me, PC)], result.at[rows_of(me * PARTS + part, PC)], own_sem.at[part]
        )
        local.start()
        local.wait()

    wait_rows(result, (CTX - 1) * OWN, back_recv)
    total = jnp.zeros((8, TOK), F32)
    for block in range(LOCAL // 128):
        rows = pl.ds(block * 128, 128)
        mix = query_t[rows, :] * result[rows, :]
        gated[rows, :] = mix
        total = total + jnp.sum((mix * mix).reshape(16, 8, TOK), axis=0)
    squares[mine] = jnp.broadcast_to(jnp.sum(total, axis=0, keepdims=True), (8, TOK))
    copies = [
        pltpu.make_async_remote_copy(
            src_ref=squares.at[mine],
            dst_ref=squares.at[mine],
            send_sem=sq_send.at[step],
            recv_sem=sq_recv.at[step],
            device_id=(me, mine ^ step),
            device_id_type=MESH,
        )
        for step in range(1, TEN)
    ]
    pl.semaphore_wait(ready.at[0], 1)
    for copy in copies:
        copy.start()
    for part in range(PARTS):
        wait_rows(sending, (CTX - 1) * PC, send_sem.at[part])
    wait_rows(sending, (CTX - 1) * OWN, back_send)

    @pl.when(first_core)
    def _():
        wait_rows(sending, (CTX // 2 - 1) * 4, filt_send)
        hand_on.wait_send()

    @pl.when(order == HALF)
    def _():
        wait_rows(sending, CTX // 2 * 4, filt_send)

    for copy in copies:
        copy.wait()
    mean = (squares[0] + squares[1] + squares[2] + squares[3]) / CHANNELS
    scale[...] = lax.rsqrt(mean + EPSILON)


def finish(mixed, scale, gain, gated_hbm, normed_hbm, gated, normed, sems):
    column = scale[...].T[:, 0:1]
    copies = []
    blocks = 4
    wide = LOCAL // blocks
    for block in range(blocks):
        columns = pl.ds(block * wide, wide)
        value = mixed[columns, :].T
        gated[:, columns] = value
        normed[:, columns] = (value * column * gain[columns].astype(F32)[None, :]).astype(BF16)
        for number, (source, target) in enumerate(((gated, gated_hbm), (normed, normed_hbm))):
            copies.append(
                pltpu.make_async_copy(source.at[:, columns], target.at[:, columns], sems.at[2 * block + number])
            )
            copies[-1].start()
    for copy in copies:
        copy.wait()


def on_device(query_gate, key_branch, value_branch, filter_spectrum, norm_gain):
    vmem = pl.BlockSpec(memory_space=pltpu.VMEM)
    constants = [jnp.asarray(table) for table in tables()]
    mixed, scale, gain = pl.pallas_call(
        mixer,
        out_shape=(
            pltpu.VMEM((LOCAL, TOK), F32),
            pltpu.VMEM((8, TOK), F32),
            pltpu.VMEM((LOCAL,), BF16),
        ),
        in_specs=[pl.BlockSpec(memory_space=pl.ANY)] * 7,
        out_specs=(vmem,) * 3,
        scratch_shapes=[
            pltpu.VMEM((TOK, LOCAL), BF16),
            pltpu.VMEM((TOK, LOCAL), BF16),
            pltpu.VMEM((TOK, LOCAL), BF16),
            pltpu.VMEM((2, 2, LOCAL // 16, TOK), F32),
            pltpu.VMEM(constants[0].shape, F32),
            pltpu.VMEM(constants[1].shape, F32),
            pltpu.SemaphoreType.DMA((7,)),
            pltpu.VMEM((256, 256), BF16),
            pltpu.VMEM((256, CTX), BF16),
            pltpu.VMEM((2, 256, 256), BF16),
            pltpu.VMEM((2, 256, 256), BF16),
            pltpu.VMEM((256, 256), BF16),
            pltpu.VMEM((LOCAL, TOK), F32),
            pltpu.VMEM((PARTS, CTX * PC, TOK), F32),
            pltpu.VMEM((PARTS, CTX * PC, TOK), F32),
            pltpu.VMEM((LOCAL, TOK), F32),
            pltpu.VMEM((LOCAL, TOK), F32),
            pltpu.VMEM((LOCAL // 16 * 4, TOK), F32),
            pltpu.VMEM(((HALF + 2) * 4, TOK), F32),
            pltpu.VMEM((PC // 2, 2 * CTX, 2 * TOK), F32),
            pltpu.VMEM((TEN, 8, TOK), F32),
            pltpu.SemaphoreType.DMA((PARTS,)),
            pltpu.SemaphoreType.DMA((PARTS,)),
            pltpu.SemaphoreType.DMA,
            pltpu.SemaphoreType.DMA,
            pltpu.SemaphoreType.DMA,
            pltpu.SemaphoreType.DMA,
            pltpu.SemaphoreType.DMA,
            pltpu.SemaphoreType.DMA((TEN,)),
            pltpu.SemaphoreType.DMA((TEN,)),
            pltpu.SemaphoreType.DMA((PARTS + 1,)),
            pltpu.SemaphoreType.REGULAR((LOW,)),
        ],
        compiler_params=pltpu.CompilerParams(
            collective_id=0, has_side_effects=True, vmem_limit_bytes=60 << 20
        ),
    )(query_gate, key_branch, value_branch, filter_spectrum.reshape(2, 2, -1, TOK), *constants, norm_gain)
    return pl.pallas_call(
        finish,
        out_shape=(
            jax.ShapeDtypeStruct((TOK, LOCAL), F32),
            jax.ShapeDtypeStruct((TOK, LOCAL), BF16),
        ),
        in_specs=[vmem] * 3,
        out_specs=(pl.BlockSpec(memory_space=pl.ANY),) * 2,
        scratch_shapes=[
            pltpu.VMEM((TOK, LOCAL), F32),
            pltpu.VMEM((TOK, LOCAL), BF16),
            pltpu.SemaphoreType.DMA((8,)),
        ],
        compiler_params=pltpu.CompilerParams(vmem_limit_bytes=16 << 20),
    )(mixed, scale, gain)


def solution(mesh):
    placed = (
        P("context", "tensor"),
        P("context", "tensor"),
        P("context", "tensor"),
        P("context", None, None, "tensor", None),
        P("tensor"),
    )
    return jax.shard_map(
        on_device,
        mesh=mesh,
        in_specs=placed,
        out_specs=(P("context", "tensor"), P("context", "tensor")),
        check_vma=False,
    )
```

```python
import functools

import jax
import jax.numpy as jnp
import numpy as np
from jax import lax
from jax.experimental import pallas as pl
from jax.experimental.pallas import tpu as pltpu
from jax.sharding import PartitionSpec as P

MESH = pl.DeviceIdType.MESH
F32, BF16 = jnp.float32, jnp.bfloat16

CHANNELS = 4096
TOK = 128
CTX = 128
TEN = 4
FREQS = 2 * TOK * CTX
LOCAL = CHANNELS // TEN
OWN = LOCAL // CTX
PARTS = 2
PC = OWN // PARTS
CHIPS = CTX // 2
PACK = 2 * PC
HALF = CTX // 2
EPSILON = 1e-06


def tables():
    f = np.concatenate([np.arange(0, CTX, 2), np.arange(1, CTX, 2)]).astype(np.float64)
    a = np.arange(CTX, dtype=np.float64)
    first = 2 * np.pi * f[:, None] * a[None, :] / (2 * CTX)
    twist = 2 * np.pi * f[:, None] * a[None, :] / FREQS
    weight = np.where(f == 0, 1.0, 2.0)[:, None] / FREQS
    edge = 2 * np.pi * CTX * a / FREQS
    turn = np.stack([np.cos(twist), np.sin(twist), np.cos(twist) * weight, np.sin(twist) * weight])
    edges = np.stack([np.cos(edge), np.sin(edge), np.cos(edge) / FREQS, np.sin(edge) / FREQS])
    edges = np.repeat(edges[:, None, :], 16, axis=1)
    second = 2 * np.pi * a[:, None] * a[None, :] / TOK
    cos, sin = np.cos(second), np.sin(second)
    forward_j = np.block([[cos, -sin], [sin, cos]])
    inverse_j = np.block([[cos, sin], [-sin, cos]])
    first = [np.concatenate([first[:, core::2], first[:, 1 - core :: 2]], axis=1) for core in (0, 1)]
    forward_a = [np.concatenate([np.cos(angle), -np.sin(angle)], axis=0) for angle in first]
    square = np.concatenate([forward_j, inverse_j, forward_a[0].T, forward_a[1].T], axis=0)
    narrow = np.concatenate([turn.reshape(-1, TOK), edges.reshape(-1, TOK), *forward_a], axis=0)
    return square.astype(np.float32), narrow.astype(np.float32)


def split(value):
    high = value.astype(BF16)
    return high, (value - high.astype(F32)).astype(BF16)


def dot(left, right):
    return jnp.dot(left, right, preferred_element_type=F32)


def three_products(value, pair):
    rows = value.shape[0]
    high, low = split(value)
    both = dot(jnp.concatenate([high, low], axis=0), pair[0])
    return both[:rows] + both[rows:] + dot(high, pair[1])


def reversed_index(position):
    flipped = 0
    for place in range(7):
        flipped = flipped + ((position >> place) & 1) * (1 << (6 - place))
    return flipped


def mixer(
    query_hbm, key_hbm, value_hbm, spectrum_hbm, square_hbm, narrow_hbm, gain_hbm,
    gated, scale, gain,
    query, key, value, spectrum, square, narrow, load_sem, a_fwd, a_low, j_fwd, j_inv, a_inv,
    sending, arrived, handed, answer, back_arrived, back_handed, result, query_t, pieces, response, transformed, squares,
    out_sem, in_sem, filt_send, filt_recv, hand_sem, sq_send, sq_recv, own_sem, ready,
):
    me = lax.axis_index("context")
    mine = lax.axis_index("tensor")
    chip, core = me // 2, me % 2

    j_rows, n_rows = 512, 4 * TOK + 64
    loads = [
        pltpu.make_async_copy(source, target, load_sem.at[number])
        for number, (source, target) in enumerate(
            [
                (key_hbm, key),
                (value_hbm, value),
                (spectrum_hbm, spectrum),
                (query_hbm, query),
                (square_hbm.at[pl.ds(0, j_rows)], square.at[pl.ds(0, j_rows)]),
                (square_hbm.at[pl.ds(j_rows + CTX * core, CTX)], square.at[pl.ds(j_rows, CTX)]),
                (narrow_hbm.at[pl.ds(0, n_rows)], narrow.at[pl.ds(0, n_rows)]),
                (narrow_hbm.at[pl.ds(n_rows + 256 * core, 256)], narrow.at[pl.ds(n_rows, 256)]),
                (gain_hbm, gain),
            ]
        )
    ]
    for load in loads:
        load.start()
    turn = [narrow.at[pl.ds(TOK * k, TOK)] for k in range(4)]
    edges = [narrow.at[pl.ds(4 * TOK + 16 * k, 16)] for k in range(4)]

    barrier = pltpu.get_barrier_semaphore()
    for step in (1, 3):
        pl.semaphore_signal(barrier, inc=1, device_id=(me, mine ^ step), device_id_type=MESH)

    def greet(other, carry):
        target = chip ^ (CHIPS - other)
        pl.semaphore_signal(barrier, inc=1, device_id=(2 * target + core, mine), device_id_type=MESH)
        return carry

    lax.fori_loop(1, CHIPS, greet, 0)
    pl.semaphore_signal(barrier, inc=1, device_id=(me ^ 1, mine), device_id_type=MESH)

    loads[0].wait()
    loads[1].wait()
    for block in range(LOCAL // 128):
        columns = pl.ds(block * 128, 128)
        driven = key[:, columns].astype(F32) * value[:, columns].astype(F32)
        driven = driven.T.reshape(8, 2, OWN, TOK)
        same = jnp.where(core == 0, driven[:, 0], driven[:, 1])
        other = jnp.where(core == 0, driven[:, 1], driven[:, 0])
        for part in range(PARTS):
            few = slice(part * PC, (part + 1) * PC)
            sending[part, pl.ds(block * 8 * PACK, 8 * PACK), :] = jnp.concatenate(
                [same[:, few], other[:, few]], axis=1
            ).reshape(8 * PACK, TOK)

    order = reversed_index(me)
    first_core = core == 0
    loads[2].wait()
    for kind in range(4):
        pieces[pl.ds(kind, LOCAL // 16, stride=4), :] = spectrum[kind // 2, kind % 2]

    pl.semaphore_wait(barrier, CHIPS - 1 + 3)
    pl.semaphore_signal(ready.at[0], inc=1, device_id=(me, mine ^ 1), device_id_type=MESH)

    @pl.when(core == 0)
    def _():
        pl.semaphore_signal(ready.at[1], inc=1, device_id=(me ^ 1, mine), device_id_type=MESH)


    def rows_of(start, count):
        return pl.ds(pl.multiple_of(start * count, count), count)

    def exchange(part, source, landing, kind):
        def step(other, carry):
            target = chip ^ (CHIPS - other) if kind == 0 else (chip + other) % CHIPS
            pltpu.make_async_remote_copy(
                src_ref=source.at[part, rows_of(target, PACK)],
                dst_ref=landing.at[part, chip],
                send_sem=out_sem.at[kind, part],
                recv_sem=in_sem.at[kind, part],
                device_id=(2 * target + core, mine),
                device_id_type=MESH,
            ).start()
            return carry

        lax.fori_loop(1, CHIPS, step, 0)
        own = pltpu.make_async_copy(
            source.at[part, rows_of(chip, PACK)], landing.at[part, chip], own_sem.at[kind // 2 * PARTS + part]
        )
        own.start()
        return own

    def hand(part, landing, target, kind):
        share = pl.ds(PC, PC)
        return pltpu.make_async_remote_copy(
            src_ref=landing.at[part, :, share],
            dst_ref=target.at[part, :, share],
            send_sem=out_sem.at[kind, part],
            recv_sem=in_sem.at[kind, part],
            device_id=(me ^ 1, mine),
            device_id_type=MESH,
        )

    def wait_blocks(ref, count, sem):
        pltpu.make_async_copy(ref.at[pl.ds(0, count)], ref.at[pl.ds(0, count)], sem).wait()

    def filter_copy(target):
        return pltpu.make_async_remote_copy(
            src_ref=pieces.at[rows_of(target, 4)],
            dst_ref=response.at[rows_of(order, 4)],
            send_sem=filt_send,
            recv_sem=filt_recv,
            device_id=(2 * target, mine),
            device_id_type=MESH,
        )

    hand_on = pltpu.make_async_remote_copy(
        src_ref=response.at[pl.ds(0, 4 * HALF + 4)],
        dst_ref=response.at[pl.ds(0, 4 * HALF + 4)],
        send_sem=hand_sem,
        recv_sem=filt_recv,
        device_id=(me ^ 1, mine),
        device_id_type=MESH,
    )

    @pl.when(first_core)
    def _():
        def step(other, carry):
            filter_copy((chip + other) % CHIPS).start()
            return carry

        lax.fori_loop(1, CHIPS, step, 0)
        local = pltpu.make_async_copy(
            pieces.at[rows_of(chip, 4)], response.at[rows_of(order, 4)], own_sem.at[2 * PARTS]
        )
        local.start()
        local.wait()

    @pl.when(jnp.logical_not(first_core))
    def _():
        pl.semaphore_wait(ready.at[1], 1)

    @pl.when(order == HALF)
    def _():
        def step(target, carry):
            filter_copy(target).start()
            return carry

        lax.fori_loop(0, CHIPS, step, 0)

    forward = [exchange(part, sending, arrived, 0) for part in range(PARTS)]
    hands = [hand(part, arrived, handed, 1) for part in range(PARTS)]

    loads[3].wait()
    for block in range(LOCAL // 128):
        columns = pl.ds(block * 128, 128)
        query_t[columns, :] = query[:, columns].astype(F32).T

    for load in loads[4:]:
        load.wait()
    for target, first in ((j_fwd, 0), (j_inv, 256)):
        target[0], target[1] = split(square[pl.ds(first, 256), :])
    a_inv[pl.ds(0, CTX), :], a_inv[pl.ds(CTX, CTX), :] = split(square[pl.ds(512, CTX), :])
    high, low = split(narrow[pl.ds(n_rows, 256), :])
    a_fwd[:, :CTX], a_fwd[:, CTX:], a_low[...] = high, high, low
    parity = jnp.where(core == 0, 1.0, -1.0)

    backward = []
    for part in range(PARTS):
        forward[part].wait()
        wait_blocks(arrived.at[part], CHIPS - 1, in_sem.at[0, part])
        hands[part].start()
        if part == 0:

            @pl.when(first_core)
            def _():
                wait_blocks(response, HALF * 4, filt_recv)
                hand_on.start()

        hands[part].wait_recv()

        edge = jnp.sum(arrived[part, :, pl.ds(0, PC), :], axis=0) - jnp.sum(handed[part, :, pl.ds(PC, PC), :], axis=0)
        edge = jnp.concatenate([edge * parity, jnp.zeros((16 - PC, TOK), F32)], axis=0)
        edge = jnp.concatenate([edge * edges[0][...], -edge * edges[1][...]], axis=1)
        edge = three_products(edge, j_fwd)

        near = arrived.at[part].reshape(CHIPS * PACK, TOK)
        far = handed.at[part].reshape(CHIPS * PACK, TOK)
        for pair in range(PC // 2):
            columns = []
            for k in (0, 1):
                channel = 2 * pair + k
                columns.append(
                    jnp.concatenate(
                        [
                            near[pl.ds(channel, CHIPS, stride=PACK), :],
                            far[pl.ds(PC + channel, CHIPS, stride=PACK), :],
                        ],
                        axis=0,
                    )
                )
            high, low = split(jnp.concatenate(columns, axis=1))
            freq = dot(a_fwd[...], jnp.concatenate([high, low], axis=0)) + dot(a_low[...], high)
            rows = []
            for k in (0, 1):
                y_re, y_im = freq[:CTX, k * TOK : (k + 1) * TOK], freq[CTX:, k * TOK : (k + 1) * TOK]
                rows.append(
                    jnp.concatenate(
                        [y_re * turn[0][...] + y_im * turn[1][...], y_im * turn[0][...] - y_re * turn[1][...]],
                        axis=1,
                    )
                )
            transformed[pair] = three_products(jnp.concatenate(rows, axis=0), j_fwd)

        if part == 0:

            @pl.when(jnp.logical_not(first_core))
            def _():
                wait_blocks(response, (HALF + 1) * 4, filt_recv)

        h_re = jnp.concatenate([response[pl.ds(kind, HALF, stride=4), :] for kind in (0, 1)], axis=0)
        h_im = jnp.concatenate([response[pl.ds(kind, HALF, stride=4), :] for kind in (2, 3)], axis=0)
        e_re, e_im = response[pl.ds(4 * HALF, 1), :], response[pl.ds(4 * HALF + 2, 1), :]
        z_re, z_im = edge[:, :TOK], edge[:, TOK:]
        edge = jnp.concatenate([z_re * e_re - z_im * e_im, z_re * e_im + z_im * e_re], axis=1)
        edge = three_products(edge, j_inv)
        edge = (edge[:, :TOK] * edges[2][...] - edge[:, TOK:] * edges[3][...]) * parity

        for pair in range(PC // 2):
            rows = []
            for k in (0, 1):
                z_re = transformed[pair, pl.ds(k * CTX, CTX), pl.ds(0, TOK)]
                z_im = transformed[pair, pl.ds(k * CTX, CTX), pl.ds(TOK, TOK)]
                rows.append(jnp.concatenate([z_re * h_re - z_im * h_im, z_re * h_im + z_im * h_re], axis=1))
            back = three_products(jnp.concatenate(rows, axis=0), j_inv)
            columns = []
            for k in (0, 1):
                u_re, u_im = back[k * CTX : (k + 1) * CTX, :TOK], back[k * CTX : (k + 1) * CTX, TOK:]
                columns.append(
                    jnp.concatenate(
                        [u_re * turn[2][...] - u_im * turn[3][...], u_im * turn[2][...] + u_re * turn[3][...]],
                        axis=0,
                    )
                )
            high, low = split(jnp.concatenate(columns, axis=1))
            both = dot(a_inv[...], high)
            back = both[:CTX] + both[CTX:] + dot(a_inv[pl.ds(0, CTX), :], low)
            for k in (0, 1):
                channel = 2 * pair + k
                row, wide = edge[channel : channel + 1], slice(k * TOK, (k + 1) * TOK)
                answer[part, pl.ds(channel, CHIPS, stride=PACK), :] = back[:CHIPS, wide] + row
                answer[part, pl.ds(PC + channel, CHIPS, stride=PACK), :] = back[CHIPS:, wide] - row

        backward.append(exchange(part, answer, back_arrived, 2))

    back_hands = [hand(part, back_arrived, back_handed, 3) for part in range(PARTS)]
    for part in range(PARTS):
        backward[part].wait()
        wait_blocks(back_arrived.at[part], CHIPS - 1, in_sem.at[2, part])
        back_hands[part].start()
    for part in range(PARTS):
        back_hands[part].wait_recv()

    total = jnp.zeros((8, TOK), F32)
    for block in range(LOCAL // 128):
        rows, chips = pl.ds(block * 128, 128), pl.ds(block * 8, 8)
        near = jnp.concatenate([back_arrived[part, chips, pl.ds(0, PC), :] for part in range(PARTS)], axis=1)
        far = jnp.concatenate([back_handed[part, chips, pl.ds(PC, PC), :] for part in range(PARTS)], axis=1)
        convolved = jnp.stack([jnp.where(core == 0, near, far), jnp.where(core == 0, far, near)], axis=1)
        mix = query_t[rows, :] * convolved.reshape(128, TOK)
        result[rows, :] = mix
        total = total + jnp.sum((mix * mix).reshape(16, 8, TOK), axis=0)
    squares[mine] = jnp.broadcast_to(jnp.sum(total, axis=0, keepdims=True), (8, TOK))
    copies = [
        pltpu.make_async_remote_copy(
            src_ref=squares.at[mine],
            dst_ref=squares.at[mine],
            send_sem=sq_send.at[step],
            recv_sem=sq_recv.at[step],
            device_id=(me, mine ^ step),
            device_id_type=MESH,
        )
        for step in (2, 1, 3)
    ]
    pl.semaphore_wait(ready.at[0], 1)
    for copy in copies:
        copy.start()
    for block in range(LOCAL // 128):
        rows = pl.ds(block * 128, 128)
        gated[:, rows] = result[rows, :].T
    for part in range(PARTS):
        wait_blocks(arrived.at[part], CHIPS - 1, out_sem.at[0, part])
        wait_blocks(arrived.at[part], CHIPS - 1, out_sem.at[2, part])
        hands[part].wait_send()
        back_hands[part].wait_send()

    @pl.when(first_core)
    def _():
        wait_blocks(pieces, (CHIPS - 1) * 4, filt_send)
        hand_on.wait_send()

    @pl.when(order == HALF)
    def _():
        wait_blocks(pieces, CHIPS * 4, filt_send)

    for copy in copies:
        copy.wait()
    mean = (squares[0] + squares[1] + squares[2] + squares[3]) / CHANNELS
    scale[...] = lax.rsqrt(mean + EPSILON)


def finish(gated, scale, gain, gated_hbm, normed_hbm, normed, sems):
    copies = [pltpu.make_async_copy(gated, gated_hbm, sems.at[0])]
    copies[0].start()
    column = scale[...].T[:, 0:1]
    blocks = 4
    wide = LOCAL // blocks
    for block in range(blocks):
        columns = pl.ds(block * wide, wide)
        normed[:, columns] = (gated[:, columns] * column * gain[columns].astype(F32)[None, :]).astype(BF16)
        copies.append(pltpu.make_async_copy(normed.at[:, columns], normed_hbm.at[:, columns], sems.at[block + 1]))
        copies[-1].start()
    for copy in copies:
        copy.wait()


def on_device(query_gate, key_branch, value_branch, filter_spectrum, norm_gain):
    vmem = pl.BlockSpec(memory_space=pltpu.VMEM)
    constants = [jnp.asarray(table) for table in tables()]
    mixed, scale, gain = pl.pallas_call(
        mixer,
        out_shape=(
            pltpu.VMEM((TOK, LOCAL), F32),
            pltpu.VMEM((8, TOK), F32),
            pltpu.VMEM((LOCAL,), BF16),
        ),
        in_specs=[pl.BlockSpec(memory_space=pl.ANY)] * 7,
        out_specs=(vmem,) * 3,
        scratch_shapes=[
            pltpu.VMEM((TOK, LOCAL), BF16),
            pltpu.VMEM((TOK, LOCAL), BF16),
            pltpu.VMEM((TOK, LOCAL), BF16),
            pltpu.VMEM((2, 2, LOCAL // 16, TOK), F32),
            pltpu.VMEM((512 + CTX, 256), F32),
            pltpu.VMEM((4 * TOK + 64 + 256, TOK), F32),
            pltpu.SemaphoreType.DMA((9,)),
            pltpu.VMEM((256, 256), BF16),
            pltpu.VMEM((256, CTX), BF16),
            pltpu.VMEM((2, 256, 256), BF16),
            pltpu.VMEM((2, 256, 256), BF16),
            pltpu.VMEM((256, 256), BF16),
            pltpu.VMEM((PARTS, CHIPS * PACK, TOK), F32),
            pltpu.VMEM((PARTS, CHIPS, PACK, TOK), F32),
            pltpu.VMEM((PARTS, CHIPS, PACK, TOK), F32),
            pltpu.VMEM((PARTS, CHIPS * PACK, TOK), F32),
            pltpu.VMEM((PARTS, CHIPS, PACK, TOK), F32),
            pltpu.VMEM((PARTS, CHIPS, PACK, TOK), F32),
            pltpu.VMEM((LOCAL, TOK), F32),
            pltpu.VMEM((LOCAL, TOK), F32),
            pltpu.VMEM((LOCAL // 16 * 4, TOK), F32),
            pltpu.VMEM(((HALF + 2) * 4, TOK), F32),
            pltpu.VMEM((PC // 2, 2 * CTX, 2 * TOK), F32),
            pltpu.VMEM((TEN, 8, TOK), F32),
            pltpu.SemaphoreType.DMA((4, PARTS)),
            pltpu.SemaphoreType.DMA((4, PARTS)),
            pltpu.SemaphoreType.DMA,
            pltpu.SemaphoreType.DMA,
            pltpu.SemaphoreType.DMA,
            pltpu.SemaphoreType.DMA((TEN,)),
            pltpu.SemaphoreType.DMA((TEN,)),
            pltpu.SemaphoreType.DMA((2 * PARTS + 1,)),
            pltpu.SemaphoreType.REGULAR((2,)),
        ],
        compiler_params=pltpu.CompilerParams(
            collective_id=0, has_side_effects=True, vmem_limit_bytes=60 << 20
        ),
    )(query_gate, key_branch, value_branch, filter_spectrum.reshape(2, 2, -1, TOK), *constants, norm_gain)
    return pl.pallas_call(
        finish,
        out_shape=(
            jax.ShapeDtypeStruct((TOK, LOCAL), F32),
            jax.ShapeDtypeStruct((TOK, LOCAL), BF16),
        ),
        in_specs=[vmem] * 3,
        out_specs=(pl.BlockSpec(memory_space=pl.ANY),) * 2,
        scratch_shapes=[
            pltpu.VMEM((TOK, LOCAL), BF16),
            pltpu.SemaphoreType.DMA((5,)),
        ],
        compiler_params=pltpu.CompilerParams(vmem_limit_bytes=16 << 20),
    )(mixed, scale, gain)


def solution(mesh):
    placed = (
        P("context", "tensor"),
        P("context", "tensor"),
        P("context", "tensor"),
        P("context", None, None, "tensor", None),
        P("tensor"),
    )
    return jax.shard_map(
        on_device,
        mesh=mesh,
        in_specs=placed,
        out_specs=(P("context", "tensor"), P("context", "tensor")),
        check_vma=False,
    )
```
